256 devices in a mesh: tp: 16 (over x_lo, z), sc: 16 (over x_hi, y, core).
Axes of the slice: x: 4 (x_hi: 2, x_lo: 2; x = x_hi * 2 + x_lo), y: 4, z: 8, core: 2. Of those that a mesh axis runs over, the one named last changes fastest.
Arguments:
- upstream: bfloat16 [16, 1024, 5120], P('sc', 'tp'), may hold values from -6 to 6
- inputs: bfloat16 [16, 1024, 5120], P('sc', 'tp'), may hold values from -6 to 6
- gate_pre: bfloat16 [16, 1024, 12800], P('sc', None, 'tp'), may hold values from -8 to 8
- up_pre: bfloat16 [16, 1024, 12800], P('sc', None, 'tp'), may hold values from -6 to 6
- down_weight: bfloat16 [12800, 5120], P('tp'), may hold values from -0.0546875 to 0.0546875
- proj_in: bfloat16 [5120, 64], replicated, may hold values from -0.078125 to 0.078125
- proj_out: bfloat16 [12800, 64], P('tp'), may hold values from -0.15625 to 0.15625
- queries: bfloat16 [2048, 4096], P('sc'), may hold values from -0.099609375 to 0.099609375
- owner_table: int32 [16, 1024, 1], P('sc', 'tp'), may hold values from 0 to 15; in each aligned block of 64 rows (0 to 63, 64 to 127, ..., all dimensions but the last counted through in order) at most 8 rows name the same one
Outputs:
- influence: float32 [16, 1024, 128], P('sc', 'tp')
The draws below stay inside these ranges and needn't reach their ends.
Inputs may be any that keep to these rules, and one draw needn't show every extreme that they name: `owner_table`: among the 64 rows of one device (aligned blocks in row order), no owner is named by more than 8 rows.
All inputs are finite; a program needn't handle non-finite values.
Results may differ from the reference program's by a relative error of at most 0.007.
Values may be sent and summed in bfloat16 or wider, within the bound.
No kernel may reach another device: no remote copies, remote signals or barrier semaphores. Data moves between devices by JAX's collectives and lax.ppermute only.
A program may use at most 128 MiB of HBM per device.

```python
import math
import jax
import jax.numpy as jnp
import numpy as np
from jax import lax

D = 5120
FF = 12800
R = 64
TOK_DEV = 64
QPD = 128
BATCHES = 16
ROWS = 1024
QUERIES = 2048
CAP = 8
N_TP = 16
N_SC = 16


def block_scale(key, shape, cuts, smallest, high):
    def one(dim, shards_of):
        heights = jax.random.uniform(jax.random.fold_in(jax.random.fold_in(key, 6), dim), (shards_of,), jnp.float32, smallest / len(cuts), high / len(cuts))
        return jnp.repeat(jnp.exp(heights), shape[dim] // shards_of).reshape((-1,) + (1,) * (len(shape) - dim - 1))

    factor_of = one(*cuts[0])
    for cut in cuts[1:]:
        factor_of = factor_of * one(*cut)
    return factor_of


def shared_out(stream_key, own, number, rows, amount, top, bound, lean):
    ranking = jax.random.permutation(stream_key, amount)
    heavy_load, ordinary = portions_of(amount, rows * top, bound, lean, True), portions_of(amount, rows * top, bound, lean, False)
    places = jnp.arange(amount)

    def named(lengths, offset_by):
        used = int((lengths > 0).sum())
        fixed = max(1, used // 4)
        shifted = fixed + (places - fixed + offset_by * (used - fixed)) % max(1, amount - fixed)
        return jnp.zeros((amount,), jnp.int32).at[ranking[jnp.where(places < fixed, places, shifted)]].set(jnp.asarray(lengths, jnp.int32))

    lengths = jnp.where(number % 4 == 0, named(heavy_load, number // 4), named(ordinary, number - number // 4 - 1))
    mixed = jax.random.permutation(jax.random.fold_in(own, 3), amount)
    source_of, sink = mixed[0:amount // 2 * 2:2], mixed[1:amount // 2 * 2:2]
    margin = jnp.minimum(lengths[source_of] - 1, bound - lengths[sink]) // 2
    margin = jnp.where((source_of == ranking[0]) | (sink == ranking[0]) | (lengths[sink] == 0), 0, jnp.maximum(margin, 0))
    shifted = jax.random.randint(jax.random.fold_in(own, 4), (amount // 2,), 0, 1 << 20) % (margin + 1)
    lengths = lengths.at[source_of].add(-shifted).at[sink].add(shifted)
    members = jnp.searchsorted(jnp.cumsum(lengths), jnp.arange(rows * top), side="right").astype(jnp.int32)
    grid = members.reshape(top, rows).T
    grid = grid[jax.random.permutation(jax.random.fold_in(own, 1), rows)]
    offset_by = jax.random.randint(jax.random.fold_in(own, 2), (rows, 1), 0, top)
    return jnp.take_along_axis(grid, (jnp.arange(top)[None, :] + offset_by) % top, axis=1)


def portions_of(number_of, total, limit, slope, full):
    portions = [(1 << 20) // math.isqrt(rank ** slope) + 1 for rank in range(1, number_of + 1)]
    largest = limit if full else min(limit, max(-(-total // number_of), total * portions[0] // sum(portions)))
    least = 1 if total - largest >= number_of - 1 else 0
    given, surplus = [largest] + [least] * (number_of - 1), total - largest - least * (number_of - 1)
    while surplus > 0:
        candidates = [i for i in range(1, number_of) if given[i] < largest] or [i for i in range(1, number_of) if given[i] < limit]
        whole, left = sum([portions[i] for i in candidates]), surplus
        for i in candidates:
            more = min(limit - given[i], max(1, left * portions[i] // whole), surplus)
            given[i] = given[i] + more
            surplus = surplus - more
    return np.array(given)


def scatter_about(rng, extent, width, limit, split=(), held_as=jnp.bfloat16):
    factor_of = block_scale(rng, extent, split, -0.22, 0.18) if split else 1.0
    drawn = jax.random.normal(rng, extent, jnp.float32) * width * factor_of
    return jnp.minimum(jnp.maximum(drawn, -limit), limit).astype(held_as)


def setup_inputs(seed: int = 0) -> dict:
    streams_of = jax.random.split(jax.random.key(seed), 10)
    upstream = scatter_about(streams_of[0], (BATCHES, ROWS, D), 1.0, 6.0, ((0, 16), (1, 16)))
    inputs = scatter_about(streams_of[1], (BATCHES, ROWS, D), 1.0, 6.0, ((0, 16), (1, 16)))
    gate_pre = scatter_about(streams_of[2], (BATCHES, ROWS, FF), 1.5, 8.0, ((0, 16), (2, 16)))
    up_pre = scatter_about(streams_of[3], (BATCHES, ROWS, FF), 1.0, 6.0, ((0, 16), (2, 16)))
    down_weight = scatter_about(streams_of[4], (FF, D), FF ** -0.5, 0.0546875, ((0, 16),))
    proj_in = scatter_about(streams_of[5], (D, R), D ** -0.5, 0.078125)
    proj_out = scatter_about(streams_of[6], (FF, R), (FF // 8) ** -0.5, 0.15625, ((0, 16),))
    queries = scatter_about(streams_of[7], (QUERIES, R * R), 0.015625, 0.099609375, ((0, 16),))
    owner_table_keys = jax.random.split(jax.random.fold_in(streams_of[8], 1), BATCHES * ROWS // TOK_DEV)
    owner_table_turns = jax.random.permutation(jax.random.fold_in(streams_of[8], 3), BATCHES * ROWS // TOK_DEV)
    owner_table = jax.vmap(lambda own, number: shared_out(jax.random.fold_in(streams_of[8], 2), own, number, TOK_DEV, N_SC, 1, CAP, 2))(owner_table_keys, owner_table_turns).reshape((BATCHES, ROWS, 1))
    return {"upstream": upstream, "inputs": inputs, "gate_pre": gate_pre, "up_pre": up_pre, "down_weight": down_weight, "proj_in": proj_in, "proj_out": proj_out, "queries": queries, "owner_table": owner_table}


def batch_factors(upstream_rows, input_rows, gate_rows, up_rows, down_weight, proj_in, proj_out):
    hidden_grad = lax.dot_general(upstream_rows, down_weight, (((1,), (1,)), ((), ())), preferred_element_type=jnp.float32)
    gate_val = gate_rows.astype(jnp.float32)
    sigmoid_val = jax.nn.sigmoid(gate_val)
    gate_grad = (hidden_grad * up_rows.astype(jnp.float32) * sigmoid_val * (1.0 + gate_val * (1.0 - sigmoid_val))).astype(jnp.bfloat16)
    out_factor = jnp.dot(gate_grad, proj_out, preferred_element_type=jnp.float32).astype(jnp.bfloat16)
    in_factor = jnp.dot(input_rows, proj_in, preferred_element_type=jnp.float32).astype(jnp.bfloat16)
    return out_factor, in_factor


def reference(upstream, inputs, gate_pre, up_pre, down_weight, proj_in, proj_out, queries, owner_table):
    def one_batch(items):
        return batch_factors(items[0], items[1], items[2], items[3], down_weight, proj_in, proj_out)

    out_factor, in_factor = lax.map(one_batch, (upstream, inputs, gate_pre, up_pre))
    row_total = BATCHES * ROWS
    flat_out = out_factor.reshape(row_total, R)
    flat_in = in_factor.reshape(row_total, R)
    owners = owner_table.reshape(row_total)
    bound_rows = CAP * N_TP * N_SC
    results = jnp.zeros((row_total, QPD), jnp.float32)
    for holder in range(N_SC):
        chosen = jnp.nonzero(owners == holder, size=bound_rows, fill_value=row_total)[0].astype(jnp.int32)
        clipped = jnp.minimum(chosen, row_total - 1)
        out_rows = flat_out[clipped]
        in_rows = flat_in[clipped]
        block = queries[holder * QPD:(holder + 1) * QPD].reshape(QPD * R, R)
        partial_q = lax.dot_general(block, in_rows, (((1,), (1,)), ((), ())), preferred_element_type=jnp.float32)
        scores = jnp.einsum("qim,mi->mq", partial_q.reshape(QPD, R, bound_rows), out_rows.astype(jnp.float32))
        results = results.at[chosen].set(scores, mode="drop")
    return results.reshape(BATCHES, ROWS, QPD)
```

```python
import functools

import jax
import jax.numpy as jnp
from jax import lax
from jax.experimental import pallas as pl
from jax.experimental.pallas import tpu as pltpu
from jax.sharding import PartitionSpec as P

NZ, NY, CAP = 8, 4, 8
F32, BF16 = jnp.float32, jnp.bfloat16


def tp_perm(flip_x, dz):
    return [
        (x * NZ + z, (x ^ flip_x) * NZ + (z + dz) % NZ) for x in range(2) for z in range(NZ)
    ]


def sc_perm(dy, flip_core):
    return [
        ((h * NY + y) * 2 + c, (h * NY + (y + dy) % NY) * 2 + (c ^ flip_core))
        for h in range(2)
        for y in range(NY)
        for c in range(2)
    ]


def along_tp(a, flip_x, dz):
    return lax.ppermute(a, "tp", tp_perm(flip_x, dz))


def along_sc(a, dy, flip_core):
    return lax.ppermute(a, "sc", sc_perm(dy, flip_core))


def across_x(a):
    pairs = []
    for x in range(2):
        for z in range(NZ):
            for s in range(16):
                pairs.append(((x * NZ + z) * 16 + s, ((1 - x) * NZ + z) * 16 + (s ^ 8)))
    return lax.ppermute(a, ("tp", "sc"), pairs)


def query_kernel(rows_ref, own_ref, other_ref, out_ref):
    count = rows_ref.shape[0]
    width = rows_ref.shape[1]
    rows = rows_ref[...]
    zeros = jnp.zeros_like(rows)
    pair = jnp.concatenate(
        [jnp.concatenate([rows, zeros], axis=1), jnp.concatenate([zeros, rows], axis=1)], axis=0
    )
    other = (lax.broadcasted_iota(jnp.int32, (2 * count, 1), 0) // CAP) % 2 == 1
    queries = own_ref.shape[0]
    dims = (((1,), (1,)), ((), ()))
    for p in range(own_ref.shape[1] // (2 * width)):
        cols = slice(p * 2 * width, (p + 1) * 2 * width)
        mine = lax.dot_general(pair, own_ref[:, cols], dims, preferred_element_type=F32)
        far = lax.dot_general(pair, other_ref[:, cols], dims, preferred_element_type=F32)
        both = jnp.where(other, far, mine).astype(BF16)
        out_ref[:, (2 * p) * queries : (2 * p + 1) * queries] = both[:count]
        out_ref[:, (2 * p + 1) * queries : (2 * p + 2) * queries] = both[count:]


def contract_queries(rows, own, other):
    count, width = rows.shape
    queries, total = own.shape
    steps = 8
    return pl.pallas_call(
        query_kernel,
        grid=(steps,),
        in_specs=[
            pl.BlockSpec((count, width), lambda p: (0, 0)),
            pl.BlockSpec((queries, total // steps), lambda p: (0, p)),
            pl.BlockSpec((queries, total // steps), lambda p: (0, p)),
        ],
        out_specs=pl.BlockSpec((count, queries * width // steps), lambda p: (0, p)),
        out_shape=jax.ShapeDtypeStruct((count, queries * width), BF16),
        compiler_params=pltpu.CompilerParams(vmem_limit_bytes=32 * 1024 * 1024),
        cost_estimate=pl.CostEstimate(
            flops=8 * count * queries * total, bytes_accessed=6 * 1024 * 1024, transcendentals=0
        ),
        name="contract_queries",
    )(rows, own, other)


def score_kernel(parts_ref, mats_ref, out_ref):
    total = parts_ref[0].astype(F32)
    for k in range(1, parts_ref.shape[0]):
        total = total + parts_ref[k].astype(F32)
    factor = total.astype(BF16).astype(F32)
    queries = out_ref.shape[1]
    score = jnp.zeros(out_ref.shape, F32)
    for i in range(factor.shape[1]):
        score = score + factor[:, i : i + 1] * mats_ref[:, i * queries : (i + 1) * queries].astype(
            F32
        )
    out_ref[...] = score


def score_rows(parts, mats):
    rows = mats.shape[0]
    queries = mats.shape[1] // parts.shape[2]
    return pl.pallas_call(
        score_kernel,
        out_shape=jax.ShapeDtypeStruct((rows, queries), F32),
        compiler_params=pltpu.CompilerParams(vmem_limit_bytes=32 * 1024 * 1024),
        name="score_rows",
    )(parts, mats)


def gating(gate, up):
    gate = gate.astype(F32)
    sig = jax.nn.sigmoid(gate)
    return (up.astype(F32) * sig * (1.0 + gate * (1.0 - sig))).astype(BF16)


def body(upstream, inputs, gate_pre, up_pre, down_weight, proj_in, proj_out, queries, owner_table):
    rows_own = upstream[0]
    count, depth = rows_own.shape
    units = down_weight.shape[0]
    column = NZ * count
    tp, sc = lax.axis_index("tp"), lax.axis_index("sc")
    x_lo, z = tp // NZ, tp % NZ
    x_hi, y, core = sc // (2 * NY), (sc // 2) % NY, sc % 2

    in_factor = jnp.dot(inputs[0], proj_in, preferred_element_type=F32).astype(BF16)
    owners = owner_table[0, :, 0]
    ids = jnp.arange(count, dtype=jnp.int32)
    same = (owners[:, None] == owners[None, :]) & (ids[:, None] > ids[None, :])
    rank = jnp.sum(same.astype(jnp.int32), axis=1)
    groups = 2 * NY
    slot = (owners % groups) * (2 * CAP) + ((owners // groups) ^ x_hi) * CAP + rank
    slots = groups * 2 * CAP
    place = (jnp.arange(slots, dtype=jnp.int32)[:, None] == slot[None, :]).astype(BF16)
    packed = jnp.dot(place, in_factor, preferred_element_type=F32).astype(BF16)
    near = [list(range(groups)), list(range(groups, 2 * groups))]
    other_queries = across_x(queries)
    arrived = lax.all_to_all(
        packed, "sc", split_axis=0, concat_axis=0, tiled=True, axis_index_groups=near
    )
    mats = contract_queries(arrived, queries, other_queries)
    mats = lax.all_to_all(
        mats, "sc", split_axis=0, concat_axis=0, tiled=True, axis_index_groups=near
    )
    own_mats = lax.dot_general(
        place, mats, (((0,), (0,)), ((), ())), preferred_element_type=F32
    ).astype(BF16)

    def half_of(a, which):
        return lax.dynamic_slice(a[0], (which * column, 0), (column, units))

    factor_own = gating(half_of(gate_pre, x_lo), half_of(up_pre, x_lo))
    factor_other = along_tp(gating(half_of(gate_pre, 1 - x_lo), half_of(up_pre, 1 - x_lo)), 1, 0)
    proj_other = along_tp(proj_out, 1, 0)
    cuts, piece = 2 * NY, depth // (2 * NY)
    half = units // 2
    weight_other = jnp.zeros((units, depth), BF16)
    for h in range(2):
        mine = lax.dynamic_slice(
            down_weight, (h * half, (y * 2 + core) * piece), (half, piece)
        )
        held = [along_tp(mine, 1, 0)]
        held.append(along_sc(held[0], 1, 0))
        held.append(along_sc(held[0], -1, 0))
        held.append(along_sc(held[1], 1, 0) if h == 0 else along_sc(held[2], -1, 0))
        for a, dy in zip(held, (0, -1, 1, 2)):
            at = ((y + dy) % NY) * 2
            weight_other = lax.dynamic_update_slice(
                weight_other, a, (h * half, (at + core) * piece)
            )
            weight_other = lax.dynamic_update_slice(
                weight_other, along_sc(a, 0, 1), (h * half, (at + 1 - core) * piece)
            )

    cut = count // 2
    up_way = {0: [rows_own[:cut], rows_own[cut:]]}
    down_way = {0: up_way[0]}
    for k in range(1, NZ // 2):
        up_way[k] = [along_tp(a, 0, 1) for a in up_way[k - 1]]
        down_way[k] = [along_tp(a, 0, -1) for a in down_way[k - 1]]
    last = [along_tp(up_way[3][0], 0, 1), along_tp(down_way[3][1], 0, -1)]
    block = {0: [rows_own], 4: last}
    for k in range(1, NZ // 2):
        block[-k] = up_way[k]
        block[k] = down_way[k]

    def factor_rows(factor, offsets):
        return jnp.concatenate(
            [
                lax.dynamic_slice(factor, (((z + o) % NZ) * count, 0), (count, units))
                for o in offsets
            ]
        )

    def grad(rows, weight, factor):
        hidden = lax.dot_general(
            rows, weight, (((1,), (1,)), ((), ())), preferred_element_type=F32
        )
        return (hidden * factor.astype(F32)).astype(BF16)

    parts = {}
    for offsets in ((0, -1, 1), (-2, 2), (-3, 3, 4)):
        rows = jnp.concatenate([a for o in offsets for a in block[o]])
        out = jnp.dot(
            grad(rows, down_weight, factor_rows(factor_own, offsets)),
            proj_out,
            preferred_element_type=F32,
        )
        out = out + jnp.dot(
            grad(rows, weight_other, factor_rows(factor_other, offsets)),
            proj_other,
            preferred_element_type=F32,
        )
        out = out.astype(BF16)
        for n, o in enumerate(offsets):
            parts[o] = out[n * count : (n + 1) * count]
    summed = jnp.stack([parts[0]] + [along_tp(parts[o], 0, o) for o in parts if o != 0])
    return score_rows(summed, own_mats)[None]


def solution(mesh):
    placed = (
        P("sc", "tp", None),
        P("sc", "tp", None),
        P("sc", None, "tp"),
        P("sc", None, "tp"),
        P("tp", None),
        P(),
        P("tp", None),
        P("sc", None),
        P("sc", "tp", None),
    )
    return jax.shard_map(
        body, mesh=mesh, in_specs=placed, out_specs=P("sc", "tp", None), check_vma=False
    )
```

```python
import functools

import jax
import jax.numpy as jnp
from jax import lax
from jax.experimental import pallas as pl
from jax.experimental.pallas import tpu as pltpu
from jax.sharding import PartitionSpec as P

NZ, NY, CAP = 8, 4, 8
F32, BF16 = jnp.float32, jnp.bfloat16
SMALL = pl.CostEstimate(flops=1000, bytes_accessed=1000, transcendentals=0)


def tp_perm(flip_x, dz):
    return [
        (x * NZ + z, (x ^ flip_x) * NZ + (z + dz) % NZ) for x in range(2) for z in range(NZ)
    ]


def sc_perm(dy, flip_core):
    return [
        ((h * NY + y) * 2 + c, (h * NY + (y + dy) % NY) * 2 + (c ^ flip_core))
        for h in range(2)
        for y in range(NY)
        for c in range(2)
    ]


def along_tp(a, flip_x, dz):
    return lax.ppermute(a, "tp", tp_perm(flip_x, dz))


def along_sc(a, dy, flip_core):
    return lax.ppermute(a, "sc", sc_perm(dy, flip_core))


def across_x(a):
    pairs = []
    for x in range(2):
        for z in range(NZ):
            for s in range(16):
                pairs.append(((x * NZ + z) * 16 + s, ((1 - x) * NZ + z) * 16 + (s ^ 8)))
    return lax.ppermute(a, ("tp", "sc"), pairs)


def query_kernel(rows_ref, own_ref, other_ref, out_ref):
    count, wide = rows_ref.shape
    rows = rows_ref[...].astype(F32).reshape(count // (2 * CAP), 2, CAP, wide)
    first = lax.broadcasted_iota(jnp.int32, (count // 2, wide), 1) < wide // 2
    queries = own_ref.shape[0]
    half = count // 2

    def doubled(a):
        a = a.reshape(half, wide)
        zeros = jnp.zeros_like(a)
        return jnp.concatenate(
            [jnp.where(first, a, zeros), jnp.where(first, zeros, a)], axis=0
        ).astype(BF16)

    near, far = doubled(rows[:, 0]), doubled(rows[:, 1])
    dims = (((1,), (1,)), ((), ()))
    for p in range(own_ref.shape[1] // wide):
        cols = slice(p * wide, (p + 1) * wide)
        a = lax.dot_general(near, own_ref[:, cols], dims, preferred_element_type=F32)
        b = lax.dot_general(far, other_ref[:, cols], dims, preferred_element_type=F32)
        for k in range(2):
            both = jnp.stack(
                [
                    a[k * half : (k + 1) * half].reshape(half // CAP, CAP, queries),
                    b[k * half : (k + 1) * half].reshape(half // CAP, CAP, queries),
                ],
                axis=1,
            ).reshape(count, queries)
            out_ref[:, (2 * p + k) * queries : (2 * p + k + 1) * queries] = both.astype(BF16)


def contract_queries(rows, own, other):
    count, wide = rows.shape
    width = wide // 2
    queries, total = own.shape
    steps = 4
    return pl.pallas_call(
        query_kernel,
        grid=(steps,),
        in_specs=[
            pl.BlockSpec((count, wide), lambda p: (0, 0)),
            pl.BlockSpec((queries, total // steps), lambda p: (0, p)),
            pl.BlockSpec((queries, total // steps), lambda p: (0, p)),
        ],
        out_specs=pl.BlockSpec((count, queries * width // steps), lambda p: (0, p)),
        out_shape=jax.ShapeDtypeStruct((count, queries * width), BF16),
        compiler_params=pltpu.CompilerParams(vmem_limit_bytes=32 * 1024 * 1024),
        cost_estimate=SMALL,
        name="contract_queries",
    )(rows, own, other)


def score_kernel(place_ref, mats_ref, parts_ref, out_ref):
    half = parts_ref.shape[0] // NZ
    total = parts_ref[:half, :].astype(F32)
    for n in range(1, NZ):
        total = total + parts_ref[n * half : (n + 1) * half, :].astype(F32)
    count = total.shape[1] // 2
    total = jnp.concatenate([total[:, :count], total[:, count:]], axis=0)
    factor = total.astype(BF16).astype(F32).T
    queries = out_ref.shape[1]
    step = 8 * queries
    score = jnp.zeros(out_ref.shape, F32)
    for first in range(0, mats_ref.shape[1], step):
        mats = jnp.dot(
            place_ref[...], mats_ref[:, first : first + step], preferred_element_type=F32
        )
        for n in range(8):
            i = first // queries + n
            score = score + factor[:, i : i + 1] * mats[:, n * queries : (n + 1) * queries]
    out_ref[...] = score


def score_rows(place, mats, parts):
    rows = place.shape[0]
    queries = mats.shape[1] // (2 * parts.shape[0] // NZ)
    return pl.pallas_call(
        score_kernel,
        out_shape=jax.ShapeDtypeStruct((rows, queries), F32),
        compiler_params=pltpu.CompilerParams(vmem_limit_bytes=16 * 1024 * 1024),
        cost_estimate=SMALL,
        name="score_rows",
    )(place, mats, parts)


UNIT_STEPS = 5


def factor_kernel(at_ref, gate_ref, up_ref, out_ref):
    gate = gate_ref[...].astype(F32)
    sig = jax.nn.sigmoid(gate)
    out_ref[...] = (up_ref[...].astype(F32) * sig * (1.0 + gate * (1.0 - sig))).astype(BF16)


def gating_factor(at, gate, up):
    units, tokens = gate.shape
    column = tokens // 2
    block = units // UNIT_STEPS
    return pl.pallas_call(
        factor_kernel,
        grid_spec=pltpu.PrefetchScalarGridSpec(
            num_scalar_prefetch=1,
            grid=(UNIT_STEPS,),
            in_specs=[pl.BlockSpec((block, column), lambda p, at: (p, at[0]))] * 2,
            out_specs=pl.BlockSpec((block, column), lambda p, at: (p, 0)),
        ),
        out_shape=jax.ShapeDtypeStruct((units, column), BF16),
        compiler_params=pltpu.CompilerParams(vmem_limit_bytes=16 * 1024 * 1024),
        cost_estimate=SMALL,
        name="gating_factor",
    )(at, gate, up)


NT = (((1,), (1,)), ((), ()))


SMEM = pl.BlockSpec(memory_space=pltpu.SMEM)
VMEM = pl.BlockSpec(memory_space=pltpu.VMEM)
HBM = pl.BlockSpec(memory_space=pltpu.HBM)


OWN_CUTS = (512, 1024, 1792, 1792)


def multiply(weight, rows, hidden, first):
    term = lax.dot_general(weight, rows, NT, preferred_element_type=F32)
    if first:
        hidden[...] = term
    else:
        hidden[...] += term


def units_kernel(at_ref, p_own, p_other, f_own, f_other, rows_hbm, own_hbm, *refs):
    weights, (out_ref, rows, own, other, factor, hidden, sems) = refs[:-7], refs[-7:]
    per, _, deep = other.shape
    piece = deep // 2
    core = at_ref[per]
    copies = []

    def copy(src, dst):
        one = pltpu.make_async_copy(src, dst, sems.at[len(copies)])
        one.start()
        copies.append(one)

    rows_cols = []
    first = 0
    for deep_n in OWN_CUTS:
        cols = pl.ds(first, deep_n)
        copy(rows_hbm.at[:, cols], rows.at[:, cols])
        copy(own_hbm.at[:, cols], own.at[:, cols])
        rows_cols.append(slice(first, first + deep_n))
        first += deep_n
    copy(f_own, factor.at[0])
    for n in range(per):
        for f in range(2):
            side = pl.ds(pl.multiple_of((core if f == 0 else 1 - core) * piece, 128), piece)
            copy(weights[f * per + n], other.at[n, :, side])
    copy(f_other, factor.at[1])
    copies = iter(copies)

    def project(k, proj):
        next(copies).wait()
        grad = (hidden[...] * factor[k].astype(F32)).astype(BF16)
        return lax.dot_general(
            proj[...], grad, (((0,), (0,)), ((), ())), preferred_element_type=F32
        )

    for n, cols in enumerate(rows_cols):
        next(copies).wait()
        next(copies).wait()
        multiply(own[:, cols], rows[:, cols], hidden, n == 0)
    total = project(0, p_own)
    for n in range(per):
        next(copies).wait()
        next(copies).wait()
        cols = pl.ds(pl.multiple_of(at_ref[n] * deep, 128), deep)
        multiply(other[n], rows[:, cols], hidden, n == 0)
    total = total + project(1, p_other)
    half = total.shape[0] // 2
    count = total.shape[1] // NZ
    for n in range(NZ):
        part = total[:, n * count : (n + 1) * count]
        part = jnp.concatenate([part[:half], part[half:]], axis=1)
        out_ref[n * half : (n + 1) * half, :] = part.astype(BF16)


def sum_units(at, p_own, p_other, f_own, f_other, rows, own, weights):
    tokens, depth = rows.shape
    units, width = p_own.shape
    return pl.pallas_call(
        units_kernel,
        in_specs=[SMEM, VMEM, VMEM] + [HBM] * (4 + len(weights)),
        out_specs=VMEM,
        out_shape=jax.ShapeDtypeStruct((NZ * width // 2, 2 * tokens // NZ), BF16),
        scratch_shapes=[
            pltpu.VMEM((tokens, depth), BF16),
            pltpu.VMEM((units, depth), BF16),
            pltpu.VMEM((NY, units, depth // NY), BF16),
            pltpu.VMEM((2, units, tokens), BF16),
            pltpu.VMEM((units, tokens), F32),
            pltpu.SemaphoreType.DMA((2 * len(OWN_CUTS) + 2 + len(weights),)),
        ],
        compiler_params=pltpu.CompilerParams(vmem_limit_bytes=56 * 1024 * 1024),
        cost_estimate=SMALL,
        name="sum_units",
    )(at, p_own, p_other, f_own, f_other, rows, own, *weights)


def together(*arrays):
    return lax.optimization_barrier(arrays)


def body(upstream, inputs, gate_pre, up_pre, down_weight, proj_in, proj_out, queries, owner_table):
    rows_own = upstream[0]
    count, depth = rows_own.shape
    units = down_weight.shape[0]
    tp, sc = lax.axis_index("tp"), lax.axis_index("sc")
    x_lo, z = tp // NZ, tp % NZ
    x_hi, y, core = sc // (2 * NY), (sc // 2) % NY, sc % 2

    columns = [list(range(NZ)), list(range(NZ, 2 * NZ))]
    rows = lax.all_gather(rows_own, "tp", axis=0, tiled=True, axis_index_groups=columns)

    piece = depth // (2 * NY)

    def eighth(column, count=units):
        return lax.dynamic_slice(down_weight, (0, column), (count, piece))

    here = along_tp(eighth((y * 2 + core) * piece), 1, 0)
    proj_other = along_tp(proj_out, 1, 0)
    other_queries = across_x(queries)
    gate, up_rows = gate_pre[0].T, up_pre[0].T
    factor_other = gating_factor(jnp.stack([1 - x_lo]), gate, up_rows)
    factor_own = gating_factor(jnp.stack([x_lo]), gate, up_rows)

    in_factor = jnp.dot(inputs[0], proj_in, preferred_element_type=F32).astype(BF16)
    at_far, in_factor = together((((y + 2) % NY) * 2 + core) * piece, in_factor)
    second = eighth(at_far)
    owners = owner_table[0, :, 0]
    ids = jnp.arange(count, dtype=jnp.int32)
    same = (owners[:, None] == owners[None, :]) & (ids[:, None] > ids[None, :])
    rank = jnp.sum(same.astype(jnp.int32), axis=1)
    groups = 2 * NY
    slot = (owners % groups) * (2 * CAP) + ((owners // groups) ^ x_hi) * CAP + rank
    slots = groups * 2 * CAP
    place = (slot[:, None] == jnp.arange(slots, dtype=jnp.int32)[None, :]).astype(BF16)
    packed = lax.dot_general(
        place,
        jnp.concatenate([in_factor, in_factor], axis=1),
        (((0,), (0,)), ((), ())),
        preferred_element_type=F32,
    ).astype(BF16)
    near = [list(range(groups)), list(range(groups, 2 * groups))]
    arrived = lax.all_to_all(
        packed, "sc", split_axis=0, concat_axis=0, tiled=True, axis_index_groups=near
    )

    here, arrived, factor_other, factor_own, second = together(
        here, arrived, factor_other, factor_own, second
    )
    before, after = along_sc(here, 1, 0), along_sc(here, -1, 0)
    factor_other = along_tp(factor_other, 1, 0)
    mats = contract_queries(arrived, queries, other_queries)

    factor_other, mats, second, proj_other = together(factor_other, mats, second, proj_other)
    far = along_tp(second, 1, 0)
    before, after, mats = together(before, after, mats)
    held = [here, before, after, far]
    flipped = [along_sc(a, 0, 1) for a in held]
    mats = lax.all_to_all(
        mats, "sc", split_axis=0, concat_axis=0, tiled=True, axis_index_groups=near
    )
    at = jnp.stack([(y + dy) % NY for dy in (0, -1, 1, 2)] + [core]).astype(jnp.int32)
    parts = sum_units(
        at,
        proj_out,
        proj_other,
        factor_own,
        factor_other,
        rows,
        down_weight,
        held + flipped,
    )
    parts, mats = together(parts, mats)
    parts = lax.all_to_all(
        parts, "tp", split_axis=0, concat_axis=0, tiled=True, axis_index_groups=columns
    )
    return score_rows(place, mats, parts)[None]


def solution(mesh):
    placed = (
        P("sc", "tp", None),
        P("sc", "tp", None),
        P("sc", None, "tp"),
        P("sc", None, "tp"),
        P("tp", None),
        P(),
        P("tp", None),
        P("sc", None),
        P("sc", "tp", None),
    )
    return jax.shard_map(
        body, mesh=mesh, in_specs=placed, out_specs=P("sc", "tp", None), check_vma=False
    )
```

```python
import functools

import jax
import jax.numpy as jnp
from jax import lax
from jax.experimental import pallas as pl
from jax.experimental.pallas import tpu as pltpu
from jax.sharding import PartitionSpec as P

NZ, NY, CAP = 8, 4, 8
F32, BF16 = jnp.float32, jnp.bfloat16
SMALL = pl.CostEstimate(flops=1000, bytes_accessed=1000, transcendentals=0)


def tp_perm(flip_x, dz):
    return [
        (x * NZ + z, (x ^ flip_x) * NZ + (z + dz) % NZ) for x in range(2) for z in range(NZ)
    ]


def sc_perm(dy, flip_core):
    return [
        ((h * NY + y) * 2 + c, (h * NY + (y + dy) % NY) * 2 + (c ^ flip_core))
        for h in range(2)
        for y in range(NY)
        for c in range(2)
    ]


def along_tp(a, flip_x, dz):
    return lax.ppermute(a, "tp", tp_perm(flip_x, dz))


def along_sc(a, dy, flip_core):
    return lax.ppermute(a, "sc", sc_perm(dy, flip_core))


def across_x(a):
    pairs = []
    for x in range(2):
        for z in range(NZ):
            for s in range(16):
                pairs.append(((x * NZ + z) * 16 + s, ((1 - x) * NZ + z) * 16 + (s ^ 8)))
    return lax.ppermute(a, ("tp", "sc"), pairs)


def query_kernel(rows_ref, own_ref, other_ref, out_ref):
    count, wide = rows_ref.shape
    rows = rows_ref[...].astype(F32).reshape(count // (2 * CAP), 2, CAP, wide)
    first = lax.broadcasted_iota(jnp.int32, (count // 2, wide), 1) < wide // 2
    queries = own_ref.shape[0]
    half = count // 2

    def doubled(a):
        a = a.reshape(half, wide)
        zeros = jnp.zeros_like(a)
        return jnp.concatenate(
            [jnp.where(first, a, zeros), jnp.where(first, zeros, a)], axis=0
        ).astype(BF16)

    near, far = doubled(rows[:, 0]), doubled(rows[:, 1])
    dims = (((1,), (1,)), ((), ()))
    for p in range(own_ref.shape[1] // wide):
        cols = slice(p * wide, (p + 1) * wide)
        a = lax.dot_general(near, own_ref[:, cols], dims, preferred_element_type=F32)
        b = lax.dot_general(far, other_ref[:, cols], dims, preferred_element_type=F32)
        for k in range(2):
            both = jnp.stack(
                [
                    a[k * half : (k + 1) * half].reshape(half // CAP, CAP, queries),
                    b[k * half : (k + 1) * half].reshape(half // CAP, CAP, queries),
                ],
                axis=1,
            ).reshape(count, queries)
            out_ref[:, (2 * p + k) * queries : (2 * p + k + 1) * queries] = both.astype(BF16)


def contract_queries(rows, own, other):
    count, wide = rows.shape
    width = wide // 2
    queries, total = own.shape
    steps = 4
    return pl.pallas_call(
        query_kernel,
        grid=(steps,),
        in_specs=[
            pl.BlockSpec((count, wide), lambda p: (0, 0)),
            pl.BlockSpec((queries, total // steps), lambda p: (0, p)),
            pl.BlockSpec((queries, total // steps), lambda p: (0, p)),
        ],
        out_specs=pl.BlockSpec((count, queries * width // steps), lambda p: (0, p)),
        out_shape=jax.ShapeDtypeStruct((count, queries * width), BF16),
        compiler_params=pltpu.CompilerParams(vmem_limit_bytes=32 * 1024 * 1024),
        cost_estimate=SMALL,
        name="contract_queries",
    )(rows, own, other)


def score_kernel(place_ref, mats_ref, parts_ref, out_ref):
    half = parts_ref.shape[0] // NZ
    total = parts_ref[:half, :].astype(F32)
    for n in range(1, NZ):
        total = total + parts_ref[n * half : (n + 1) * half, :].astype(F32)
    count = total.shape[1] // 2
    total = jnp.concatenate([total[:, :count], total[:, count:]], axis=0)
    factor = total.astype(BF16).astype(F32).T
    queries = out_ref.shape[1]
    step = 8 * queries
    score = jnp.zeros(out_ref.shape, F32)
    for first in range(0, mats_ref.shape[1], step):
        mats = jnp.dot(
            place_ref[...], mats_ref[:, first : first + step], preferred_element_type=F32
        )
        for n in range(8):
            i = first // queries + n
            score = score + factor[:, i : i + 1] * mats[:, n * queries : (n + 1) * queries]
    out_ref[...] = score


def score_rows(place, mats, parts):
    rows = place.shape[0]
    queries = mats.shape[1] // (2 * parts.shape[0] // NZ)
    return pl.pallas_call(
        score_kernel,
        out_shape=jax.ShapeDtypeStruct((rows, queries), F32),
        compiler_params=pltpu.CompilerParams(vmem_limit_bytes=16 * 1024 * 1024),
        cost_estimate=SMALL,
        name="score_rows",
    )(place, mats, parts)


UNIT_STEPS = 5


def factor_kernel(at_ref, gate_ref, up_ref, out_ref):
    gate = gate_ref[...].astype(F32)
    sig = jax.nn.sigmoid(gate)
    out = up_ref[...].astype(F32) * sig * (1.0 + gate * (1.0 - sig))
    out_ref[...] = out.astype(BF16)


def gating_factor(at, gate, up):
    units, tokens = gate.shape
    column = tokens // 2
    block = units // UNIT_STEPS
    return pl.pallas_call(
        factor_kernel,
        grid_spec=pltpu.PrefetchScalarGridSpec(
            num_scalar_prefetch=1,
            grid=(UNIT_STEPS,),
            in_specs=[pl.BlockSpec((block, column), lambda p, at: (p, at[0]))] * 2,
            out_specs=pl.BlockSpec((block, column), lambda p, at: (p, 0)),
        ),
        out_shape=jax.ShapeDtypeStruct((units, column), BF16),
        compiler_params=pltpu.CompilerParams(vmem_limit_bytes=16 * 1024 * 1024),
        cost_estimate=SMALL,
        name="gating_factor",
    )(at, gate, up)


NT = (((1,), (1,)), ((), ()))


SMEM = pl.BlockSpec(memory_space=pltpu.SMEM)
VMEM = pl.BlockSpec(memory_space=pltpu.VMEM)
HBM = pl.BlockSpec(memory_space=pltpu.HBM)


def multiply(weight, rows, hidden, first):
    term = lax.dot_general(weight, rows, NT, preferred_element_type=F32)
    if first:
        hidden[...] = term
    else:
        hidden[...] += term


def project(hidden, factor, proj):
    grad = (hidden * factor.astype(F32)).astype(BF16)
    return lax.dot_general(proj, grad, (((0,), (0,)), ((), ())), preferred_element_type=F32)


def units_kernel(at_ref, p_own, p_other, f_own, f_other, own_hbm, rows_hbm, *refs):
    weights, (out_ref, rows, own, other, factor, hidden, sems) = refs[:-7], refs[-7:]
    per, _, deep = other.shape
    side = deep // 2
    sides = [pl.ds(pl.multiple_of(at_ref[per + f] * side, 128), side) for f in range(2)]
    groups = []
    for n in range(per):
        columns = pl.ds(n * deep, deep)
        group = [(own_hbm.at[:, columns], own.at[n])]
        group.append((rows_hbm.at[:, columns], rows.at[n]))
        groups.append(group)
    groups[-1].append((f_own, factor.at[0]))
    for n in range(per):
        groups.append([(weights[2 * n + f], other.at[n, :, sides[f]]) for f in range(2)])
    groups[-1].append((f_other, factor.at[1]))
    started = []
    count = 0
    for group in groups:
        started.append([])
        for src, dst in group:
            started[-1].append(pltpu.make_async_copy(src, dst, sems.at[count]))
            count += 1

    ahead = 3
    for group in started[:ahead]:
        for one in group:
            one.start()
    total = None
    for k, group in enumerate(started):
        for one in group:
            one.wait()
        for one in started[k + ahead] if k + ahead < len(started) else []:
            one.start()
        n = k % per
        if k < per:
            multiply(own[n], rows[n], hidden, n == 0)
        else:
            multiply(other[n], rows[at_ref[n]], hidden, n == 0)
        if k == per - 1:
            total = project(hidden[...], factor[0], p_own[...])
    total = total + project(hidden[...], factor[1], p_other[...])
    half = total.shape[0] // 2
    count = total.shape[1] // NZ
    for n in range(NZ):
        part = total[:, n * count : (n + 1) * count]
        part = jnp.concatenate([part[:half], part[half:]], axis=1)
        out_ref[n * half : (n + 1) * half, :] = part.astype(BF16)


def sum_units(at, p_own, p_other, f_own, f_other, own, rows, weights):
    units, depth = own.shape
    tokens, width = f_own.shape[1], p_own.shape[1]
    deep = depth // NY
    copies = 2 * NY + 2 + len(weights)
    return pl.pallas_call(
        units_kernel,
        in_specs=[SMEM, VMEM, VMEM] + [HBM] * (4 + len(weights)),
        out_specs=VMEM,
        out_shape=jax.ShapeDtypeStruct((NZ * width // 2, 2 * tokens // NZ), BF16),
        scratch_shapes=[
            pltpu.VMEM((NY, tokens, deep), BF16),
            pltpu.VMEM((NY, units, deep), BF16),
            pltpu.VMEM((NY, units, deep), BF16),
            pltpu.VMEM((2, units, tokens), BF16),
            pltpu.VMEM((units, tokens), F32),
            pltpu.SemaphoreType.DMA((copies,)),
        ],
        compiler_params=pltpu.CompilerParams(vmem_limit_bytes=56 * 1024 * 1024),
        cost_estimate=SMALL,
        name="sum_units",
    )(at, p_own, p_other, f_own, f_other, own, rows, *weights)


def together(*arrays):
    return lax.optimization_barrier(arrays)


def body(upstream, inputs, gate_pre, up_pre, down_weight, proj_in, proj_out, queries, owner_table):
    rows_own = upstream[0]
    count, depth = rows_own.shape
    units = down_weight.shape[0]
    tp, sc = lax.axis_index("tp"), lax.axis_index("sc")
    x_lo, z = tp // NZ, tp % NZ
    x_hi, y, core = sc // (2 * NY), (sc // 2) % NY, sc % 2

    columns = [list(range(NZ)), list(range(NZ, 2 * NZ))]

    piece = depth // (2 * NY)
    rows = lax.all_gather(rows_own, "tp", axis=0, tiled=True, axis_index_groups=columns)

    def eighth(dy):
        column = (((y + dy) % NY) * 2 + core) * piece
        return lax.dynamic_slice(down_weight, (0, column), (units, piece))

    first, second = together(eighth(0), eighth(2))
    here = along_tp(first, 1, 0)
    other_queries, proj_other = across_x(queries), across_x(proj_out)

    in_factor = jnp.dot(inputs[0], proj_in, preferred_element_type=F32).astype(BF16)
    owners = owner_table[0, :, 0]
    ids = jnp.arange(count, dtype=jnp.int32)
    same = (owners[:, None] == owners[None, :]) & (ids[:, None] > ids[None, :])
    rank = jnp.sum(same.astype(jnp.int32), axis=1)
    groups = 2 * NY
    slot = (owners % groups) * (2 * CAP) + ((owners // groups) ^ x_hi) * CAP + rank
    slots = groups * 2 * CAP
    place = (slot[:, None] == jnp.arange(slots, dtype=jnp.int32)[None, :]).astype(BF16)
    packed = lax.dot_general(
        place,
        jnp.concatenate([in_factor, in_factor], axis=1),
        (((0,), (0,)), ((), ())),
        preferred_element_type=F32,
    ).astype(BF16)
    near = [list(range(groups)), list(range(groups, 2 * groups))]
    arrived = lax.all_to_all(
        packed, "sc", split_axis=0, concat_axis=0, tiled=True, axis_index_groups=near
    )

    gate, up_rows = gate_pre[0].T, up_pre[0].T
    factor_other = gating_factor(jnp.stack([1 - x_lo]), gate, up_rows)
    factor_own = gating_factor(jnp.stack([x_lo]), gate, up_rows)

    here, second, arrived, factor_other, factor_own = together(
        here, second, arrived, factor_other, factor_own
    )
    before, after = along_sc(here, 1, 0), along_sc(here, -1, 0)
    factor_other, far = along_tp(factor_other, 1, 0), across_x(second)
    mats = contract_queries(arrived, queries, other_queries)
    mats = lax.all_to_all(
        mats, "sc", split_axis=0, concat_axis=0, tiled=True, axis_index_groups=near
    )
    before, after, factor_other, far, proj_other = together(
        before, after, factor_other, far, proj_other
    )
    weights = []
    for a in (here, before, after, far):
        weights += [a, along_sc(a, 0, 1)]

    at = [(y + dy) % NY for dy in (0, -1, 1, 2)] + [core, 1 - core]
    parts = sum_units(
        jnp.stack(at).astype(jnp.int32),
        proj_out,
        proj_other,
        factor_own,
        factor_other,
        down_weight,
        rows,
        weights,
    )
    parts, mats = together(parts, mats)
    parts = lax.all_to_all(
        parts, "tp", split_axis=0, concat_axis=0, tiled=True, axis_index_groups=columns
    )
    return score_rows(place, mats, parts)[None]


def solution(mesh):
    placed = (
        P("sc", "tp", None),
        P("sc", "tp", None),
        P("sc", None, "tp"),
        P("sc", None, "tp"),
        P("tp", None),
        P(),
        P("tp", None),
        P("sc", None),
        P("sc", "tp", None),
    )
    return jax.shard_map(
        body, mesh=mesh, in_specs=placed, out_specs=P("sc", "tp", None), check_vma=False
    )
```

```python
import functools

import jax
import jax.numpy as jnp
from jax import lax
from jax.experimental import pallas as pl
from jax.experimental.pallas import tpu as pltpu
from jax.sharding import PartitionSpec as P

NZ, NY, CAP = 8, 4, 8
F32, BF16 = jnp.float32, jnp.bfloat16
SMALL = pl.CostEstimate(flops=1000, bytes_accessed=1000, transcendentals=0)


def tp_perm(flip_x, dz):
    return [
        (x * NZ + z, (x ^ flip_x) * NZ + (z + dz) % NZ) for x in range(2) for z in range(NZ)
    ]


def sc_perm(dy, flip_core):
    return [
        ((h * NY + y) * 2 + c, (h * NY + (y + dy) % NY) * 2 + (c ^ flip_core))
        for h in range(2)
        for y in range(NY)
        for c in range(2)
    ]


def along_tp(a, flip_x, dz):
    return lax.ppermute(a, "tp", tp_perm(flip_x, dz))


def along_sc(a, dy, flip_core):
    return lax.ppermute(a, "sc", sc_perm(dy, flip_core))


def across_x(a):
    pairs = []
    for x in range(2):
        for z in range(NZ):
            for s in range(16):
                pairs.append(((x * NZ + z) * 16 + s, ((1 - x) * NZ + z) * 16 + (s ^ 8)))
    return lax.ppermute(a, ("tp", "sc"), pairs)


def query_kernel(rows_ref, own_ref, other_ref, out_ref):
    count, wide = rows_ref.shape
    rows = rows_ref[...].astype(F32).reshape(count // (2 * CAP), 2, CAP, wide)
    first = lax.broadcasted_iota(jnp.int32, (count // 2, wide), 1) < wide // 2
    queries = own_ref.shape[0]
    half = count // 2

    def doubled(a):
        a = a.reshape(half, wide)
        zeros = jnp.zeros_like(a)
        return jnp.concatenate(
            [jnp.where(first, a, zeros), jnp.where(first, zeros, a)], axis=0
        ).astype(BF16)

    near, far = doubled(rows[:, 0]), doubled(rows[:, 1])
    dims = (((1,), (1,)), ((), ()))
    for p in range(own_ref.shape[1] // wide):
        cols = slice(p * wide, (p + 1) * wide)
        a = lax.dot_general(near, own_ref[:, cols], dims, preferred_element_type=F32)
        b = lax.dot_general(far, other_ref[:, cols], dims, preferred_element_type=F32)
        for k in range(2):
            both = jnp.stack(
                [
                    a[k * half : (k + 1) * half].reshape(half // CAP, CAP, queries),
                    b[k * half : (k + 1) * half].reshape(half // CAP, CAP, queries),
                ],
                axis=1,
            ).reshape(count, queries)
            out_ref[:, (2 * p + k) * queries : (2 * p + k + 1) * queries] = both.astype(BF16)


def contract_queries(rows, own, other):
    count, wide = rows.shape
    width = wide // 2
    queries, total = own.shape
    steps = 4
    return pl.pallas_call(
        query_kernel,
        grid=(steps,),
        in_specs=[
            pl.BlockSpec((count, wide), lambda p: (0, 0)),
            pl.BlockSpec((queries, total // steps), lambda p: (0, p)),
            pl.BlockSpec((queries, total // steps), lambda p: (0, p)),
        ],
        out_specs=pl.BlockSpec((count, queries * width // steps), lambda p: (0, p)),
        out_shape=jax.ShapeDtypeStruct((count, queries * width), BF16),
        compiler_params=pltpu.CompilerParams(vmem_limit_bytes=32 * 1024 * 1024),
        cost_estimate=SMALL,
        name="contract_queries",
    )(rows, own, other)


def score_kernel(mats_ref, parts_ref, out_ref):
    half = parts_ref.shape[0] // NZ
    total = parts_ref[:half, :].astype(F32)
    for n in range(1, NZ):
        total = total + parts_ref[n * half : (n + 1) * half, :].astype(F32)
    count = total.shape[1] // 2
    total = jnp.concatenate([total[:, :count], total[:, count:]], axis=0)
    factor = total.astype(BF16).astype(F32).T
    queries = out_ref.shape[1]
    score = jnp.zeros(out_ref.shape, F32)
    for i in range(factor.shape[1]):
        mats = mats_ref[:, i * queries : (i + 1) * queries].astype(F32)
        score = score + factor[:, i : i + 1] * mats
    out_ref[...] = score


def score_rows(mats, parts):
    rows = mats.shape[0]
    queries = mats.shape[1] // (2 * parts.shape[0] // NZ)
    return pl.pallas_call(
        score_kernel,
        out_shape=jax.ShapeDtypeStruct((rows, queries), F32),
        compiler_params=pltpu.CompilerParams(vmem_limit_bytes=16 * 1024 * 1024),
        cost_estimate=SMALL,
        name="score_rows",
    )(mats, parts)


UNIT_STEPS = 5


def factor_kernel(at_ref, gate_ref, up_ref, out_ref):
    gate = gate_ref[...].astype(F32)
    sig = jax.nn.sigmoid(gate)
    out = up_ref[...].astype(F32) * sig * (1.0 + gate * (1.0 - sig))
    out_ref[...] = out.astype(BF16)


def gating_factor(at, gate, up):
    units, tokens = gate.shape
    column = tokens // 2
    block = units // UNIT_STEPS
    return pl.pallas_call(
        factor_kernel,
        grid_spec=pltpu.PrefetchScalarGridSpec(
            num_scalar_prefetch=1,
            grid=(UNIT_STEPS,),
            in_specs=[pl.BlockSpec((block, column), lambda p, at: (p, at[0]))] * 2,
            out_specs=pl.BlockSpec((block, column), lambda p, at: (p, 0)),
        ),
        out_shape=jax.ShapeDtypeStruct((units, column), BF16),
        compiler_params=pltpu.CompilerParams(vmem_limit_bytes=16 * 1024 * 1024),
        cost_estimate=SMALL,
        name="gating_factor",
    )(at, gate, up)


NT = (((1,), (1,)), ((), ()))


SMEM = pl.BlockSpec(memory_space=pltpu.SMEM)
VMEM = pl.BlockSpec(memory_space=pltpu.VMEM)
HBM = pl.BlockSpec(memory_space=pltpu.HBM)


def multiply(weight, rows, hidden, first):
    term = lax.dot_general(weight, rows, NT, preferred_element_type=F32)
    if first:
        hidden[...] = term
    else:
        hidden[...] += term


def project(hidden, factor, proj):
    grad = (hidden * factor.astype(F32)).astype(BF16)
    return lax.dot_general(proj, grad, (((0,), (0,)), ((), ())), preferred_element_type=F32)


def units_kernel(at_ref, p_own, p_other, f_own, f_other, own_hbm, rows_hbm, *refs):
    weights, (out_ref, rows, own, other, factor, hidden, sems) = refs[:-7], refs[-7:]
    per, _, deep = other.shape
    side = deep // 2
    sides = [pl.ds(pl.multiple_of(at_ref[per + f] * side, 128), side) for f in range(2)]
    groups = []
    for n in range(per):
        columns = pl.ds(n * deep, deep)
        group = [(own_hbm.at[:, columns], own.at[n])]
        group.append((rows_hbm.at[:, columns], rows.at[n]))
        groups.append(group)
    groups[-1].append((f_own, factor.at[0]))
    for n in range(per):
        groups.append([(weights[2 * n + f], other.at[n, :, sides[f]]) for f in range(2)])
    groups[-1].append((f_other, factor.at[1]))
    started = []
    count = 0
    for group in groups:
        started.append([])
        for src, dst in group:
            started[-1].append(pltpu.make_async_copy(src, dst, sems.at[count]))
            count += 1

    ahead = 3
    for group in started[:ahead]:
        for one in group:
            one.start()
    total = None
    for k, group in enumerate(started):
        for one in group:
            one.wait()
        for one in started[k + ahead] if k + ahead < len(started) else []:
            one.start()
        n = k % per
        if k < per:
            multiply(own[n], rows[n], hidden, n == 0)
        else:
            multiply(other[n], rows[at_ref[n]], hidden, n == 0)
        if k == per - 1:
            total = project(hidden[...], factor[0], p_own[...])
    total = total + project(hidden[...], factor[1], p_other[...])
    half = total.shape[0] // 2
    count = total.shape[1] // NZ
    for n in range(NZ):
        part = total[:, n * count : (n + 1) * count]
        part = jnp.concatenate([part[:half], part[half:]], axis=1)
        out_ref[n * half : (n + 1) * half, :] = part.astype(BF16)


def sum_units(at, p_own, p_other, f_own, f_other, own, rows, weights):
    units, depth = own.shape
    tokens, width = f_own.shape[1], p_own.shape[1]
    deep = depth // NY
    copies = 2 * NY + 2 + len(weights)
    return pl.pallas_call(
        units_kernel,
        in_specs=[SMEM, VMEM, VMEM] + [HBM] * (4 + len(weights)),
        out_specs=VMEM,
        out_shape=jax.ShapeDtypeStruct((NZ * width // 2, 2 * tokens // NZ), BF16),
        scratch_shapes=[
            pltpu.VMEM((NY, tokens, deep), BF16),
            pltpu.VMEM((NY, units, deep), BF16),
            pltpu.VMEM((NY, units, deep), BF16),
            pltpu.VMEM((2, units, tokens), BF16),
            pltpu.VMEM((units, tokens), F32),
            pltpu.SemaphoreType.DMA((copies,)),
        ],
        compiler_params=pltpu.CompilerParams(vmem_limit_bytes=56 * 1024 * 1024),
        cost_estimate=SMALL,
        name="sum_units",
    )(at, p_own, p_other, f_own, f_other, own, rows, *weights)


def together(*arrays):
    return lax.optimization_barrier(arrays)


def body(upstream, inputs, gate_pre, up_pre, down_weight, proj_in, proj_out, queries, owner_table):
    rows_own = upstream[0]
    count, depth = rows_own.shape
    units = down_weight.shape[0]
    tp, sc = lax.axis_index("tp"), lax.axis_index("sc")
    x_lo, z = tp // NZ, tp % NZ
    x_hi, y, core = sc // (2 * NY), (sc // 2) % NY, sc % 2

    columns = [list(range(NZ)), list(range(NZ, 2 * NZ))]

    piece = depth // (2 * NY)
    rows = lax.all_gather(rows_own, "tp", axis=0, tiled=True, axis_index_groups=columns)

    def eighth(dy):
        column = (((y + dy) % NY) * 2 + core) * piece
        return lax.dynamic_slice(down_weight, (0, column), (units, piece))

    first, second = together(eighth(0), eighth(2))
    here = along_tp(first, 1, 0)
    other_queries, proj_other = across_x(queries), across_x(proj_out)

    in_factor = jnp.dot(inputs[0], proj_in, preferred_element_type=F32).astype(BF16)
    owners = owner_table[0, :, 0]
    ids = jnp.arange(count, dtype=jnp.int32)
    same = (owners[:, None] == owners[None, :]) & (ids[:, None] > ids[None, :])
    rank = jnp.sum(same.astype(jnp.int32), axis=1)
    groups = 2 * NY
    slot = (owners % groups) * (2 * CAP) + ((owners // groups) ^ x_hi) * CAP + rank
    slots = groups * 2 * CAP
    place = (slot[:, None] == jnp.arange(slots, dtype=jnp.int32)[None, :]).astype(BF16)
    packed = lax.dot_general(
        place,
        jnp.concatenate([in_factor, in_factor], axis=1),
        (((0,), (0,)), ((), ())),
        preferred_element_type=F32,
    ).astype(BF16)
    near = [list(range(groups)), list(range(groups, 2 * groups))]
    arrived = lax.all_to_all(
        packed, "sc", split_axis=0, concat_axis=0, tiled=True, axis_index_groups=near
    )

    gate, up_rows = gate_pre[0].T, up_pre[0].T
    factor_other = gating_factor(jnp.stack([1 - x_lo]), gate, up_rows)
    factor_own = gating_factor(jnp.stack([x_lo]), gate, up_rows)

    here, second, arrived, factor_other, factor_own = together(
        here, second, arrived, factor_other, factor_own
    )
    before, after = along_sc(here, 1, 0), along_sc(here, -1, 0)
    factor_other, far = along_tp(factor_other, 1, 0), across_x(second)
    mats = contract_queries(arrived, queries, other_queries)
    mats = lax.all_to_all(
        mats, "sc", split_axis=0, concat_axis=0, tiled=True, axis_index_groups=near
    )
    before, after, factor_other, far, proj_other = together(
        before, after, factor_other, far, proj_other
    )
    weights = []
    for a in (here, before, after, far):
        weights += [a, along_sc(a, 0, 1)]

    at = [(y + dy) % NY for dy in (0, -1, 1, 2)] + [core, 1 - core]
    parts = sum_units(
        jnp.stack(at).astype(jnp.int32),
        proj_out,
        proj_other,
        factor_own,
        factor_other,
        down_weight,
        rows,
        weights,
    )
    parts, mats = together(parts, mats)
    parts = lax.all_to_all(
        parts, "tp", split_axis=0, concat_axis=0, tiled=True, axis_index_groups=columns
    )
    mats = jnp.dot(place, mats, preferred_element_type=F32).astype(BF16)
    return score_rows(mats, parts)[None]


def solution(mesh):
    placed = (
        P("sc", "tp", None),
        P("sc", "tp", None),
        P("sc", None, "tp"),
        P("sc", None, "tp"),
        P("tp", None),
        P(),
        P("tp", None),
        P("sc", None),
        P("sc", "tp", None),
    )
    return jax.shard_map(
        body, mesh=mesh, in_specs=placed, out_specs=P("sc", "tp", None), check_vma=False
    )
```

```python
import functools

import jax
import jax.numpy as jnp
from jax import lax
from jax.experimental import pallas as pl
from jax.experimental.pallas import tpu as pltpu
from jax.sharding import PartitionSpec as P

NZ, NY, CAP = 8, 4, 8
F32, BF16 = jnp.float32, jnp.bfloat16
SMALL = pl.CostEstimate(flops=1000, bytes_accessed=1000, transcendentals=0)


def tp_perm(flip_x, dz):
    return [
        (x * NZ + z, (x ^ flip_x) * NZ + (z + dz) % NZ) for x in range(2) for z in range(NZ)
    ]


def sc_perm(dy, flip_core):
    return [
        ((h * NY + y) * 2 + c, (h * NY + (y + dy) % NY) * 2 + (c ^ flip_core))
        for h in range(2)
        for y in range(NY)
        for c in range(2)
    ]


def along_tp(a, flip_x, dz):
    return lax.ppermute(a, "tp", tp_perm(flip_x, dz))


def along_sc(a, dy, flip_core):
    return lax.ppermute(a, "sc", sc_perm(dy, flip_core))


def across_x(a):
    pairs = []
    for x in range(2):
        for z in range(NZ):
            for s in range(16):
                pairs.append(((x * NZ + z) * 16 + s, ((1 - x) * NZ + z) * 16 + (s ^ 8)))
    return lax.ppermute(a, ("tp", "sc"), pairs)


def query_kernel(rows_ref, own_ref, other_ref, out_ref):
    count, wide = rows_ref.shape
    rows = rows_ref[...].astype(F32).reshape(count // (2 * CAP), 2, CAP, wide)
    first = lax.broadcasted_iota(jnp.int32, (count // 2, wide), 1) < wide // 2
    queries = own_ref.shape[0]
    half = count // 2

    def doubled(a):
        a = a.reshape(half, wide)
        zeros = jnp.zeros_like(a)
        return jnp.concatenate(
            [jnp.where(first, a, zeros), jnp.where(first, zeros, a)], axis=0
        ).astype(BF16)

    near, far = doubled(rows[:, 0]), doubled(rows[:, 1])
    dims = (((1,), (1,)), ((), ()))
    for p in range(own_ref.shape[1] // wide):
        cols = slice(p * wide, (p + 1) * wide)
        a = lax.dot_general(near, own_ref[:, cols], dims, preferred_element_type=F32)
        b = lax.dot_general(far, other_ref[:, cols], dims, preferred_element_type=F32)
        for k in range(2):
            both = jnp.stack(
                [
                    a[k * half : (k + 1) * half].reshape(half // CAP, CAP, queries),
                    b[k * half : (k + 1) * half].reshape(half // CAP, CAP, queries),
                ],
                axis=1,
            ).reshape(count, queries)
            out_ref[:, (2 * p + k) * queries : (2 * p + k + 1) * queries] = both.astype(BF16)


def contract_queries(rows, own, other):
    count, wide = rows.shape
    width = wide // 2
    queries, total = own.shape
    steps = 4
    return pl.pallas_call(
        query_kernel,
        grid=(steps,),
        in_specs=[
            pl.BlockSpec((count, wide), lambda p: (0, 0)),
            pl.BlockSpec((queries, total // steps), lambda p: (0, p)),
            pl.BlockSpec((queries, total // steps), lambda p: (0, p)),
        ],
        out_specs=pl.BlockSpec((count, queries * width // steps), lambda p: (0, p)),
        out_shape=jax.ShapeDtypeStruct((count, queries * width), BF16),
        compiler_params=pltpu.CompilerParams(vmem_limit_bytes=32 * 1024 * 1024),
        cost_estimate=SMALL,
        name="contract_queries",
    )(rows, own, other)


def score_kernel(place_ref, mats_ref, parts_ref, out_ref):
    half = parts_ref.shape[0] // NZ
    total = parts_ref[:half, :].astype(F32)
    for n in range(1, NZ):
        total = total + parts_ref[n * half : (n + 1) * half, :].astype(F32)
    count = total.shape[1] // 2
    total = jnp.concatenate([total[:, :count], total[:, count:]], axis=0)
    factor = total.astype(BF16).astype(F32).T
    queries = out_ref.shape[1]
    step = 8 * queries
    score = jnp.zeros(out_ref.shape, F32)
    for first in range(0, mats_ref.shape[1], step):
        mats = jnp.dot(
            place_ref[...], mats_ref[:, first : first + step], preferred_element_type=F32
        )
        for n in range(8):
            i = first // queries + n
            score = score + factor[:, i : i + 1] * mats[:, n * queries : (n + 1) * queries]
    out_ref[...] = score


def score_rows(place, mats, parts):
    rows = place.shape[0]
    queries = mats.shape[1] // (2 * parts.shape[0] // NZ)
    return pl.pallas_call(
        score_kernel,
        out_shape=jax.ShapeDtypeStruct((rows, queries), F32),
        compiler_params=pltpu.CompilerParams(vmem_limit_bytes=16 * 1024 * 1024),
        cost_estimate=SMALL,
        name="score_rows",
    )(place, mats, parts)


UNIT_STEPS = 5


def factor_kernel(at_ref, gate_ref, up_ref, out_ref):
    gate = gate_ref[...].astype(F32)
    sig = jax.nn.sigmoid(gate)
    out = up_ref[...].astype(F32) * sig * (1.0 + gate * (1.0 - sig))
    out_ref[...] = out.astype(BF16)


def gating_factor(at, gate, up):
    units, tokens = gate.shape
    column = tokens // 2
    block = units // UNIT_STEPS
    return pl.pallas_call(
        factor_kernel,
        grid_spec=pltpu.PrefetchScalarGridSpec(
            num_scalar_prefetch=1,
            grid=(UNIT_STEPS,),
            in_specs=[pl.BlockSpec((block, column), lambda p, at: (p, at[0]))] * 2,
            out_specs=pl.BlockSpec((block, column), lambda p, at: (p, 0)),
        ),
        out_shape=jax.ShapeDtypeStruct((units, column), BF16),
        compiler_params=pltpu.CompilerParams(vmem_limit_bytes=16 * 1024 * 1024),
        cost_estimate=SMALL,
        name="gating_factor",
    )(at, gate, up)


NT = (((1,), (1,)), ((), ()))


SMEM = pl.BlockSpec(memory_space=pltpu.SMEM)
VMEM = pl.BlockSpec(memory_space=pltpu.VMEM)
HBM = pl.BlockSpec(memory_space=pltpu.HBM)


def multiply(weight, rows, hidden, first):
    term = lax.dot_general(weight, rows, NT, preferred_element_type=F32)
    if first:
        hidden[...] = term
    else:
        hidden[...] += term


def project(hidden, factor, proj):
    grad = (hidden * factor.astype(F32)).astype(BF16)
    return lax.dot_general(proj, grad, (((0,), (0,)), ((), ())), preferred_element_type=F32)


def units_kernel(at_ref, p_own, p_other, f_own, f_other, own_hbm, rows_hbm, *refs):
    weights, (out_ref, rows, own, other, factor, hidden, sems) = refs[:-7], refs[-7:]
    per, _, deep = other.shape
    side = deep // 2
    sides = [pl.ds(pl.multiple_of(at_ref[per + f] * side, 128), side) for f in range(2)]
    groups = []
    for n in range(per):
        columns = pl.ds(n * deep, deep)
        group = [(own_hbm.at[:, columns], own.at[n])]
        group.append((rows_hbm.at[:, columns], rows.at[n]))
        groups.append(group)
    groups[-1].append((f_own, factor.at[0]))
    for n in range(per):
        groups.append([(weights[2 * n + f], other.at[n, :, sides[f]]) for f in range(2)])
    groups[-1].append((f_other, factor.at[1]))
    started = []
    count = 0
    for group in groups:
        started.append([])
        for src, dst in group:
            started[-1].append(pltpu.make_async_copy(src, dst, sems.at[count]))
            count += 1

    ahead = 3
    for group in started[:ahead]:
        for one in group:
            one.start()
    total = None
    for k, group in enumerate(started):
        for one in group:
            one.wait()
        for one in started[k + ahead] if k + ahead < len(started) else []:
            one.start()
        n = k % per
        if k < per:
            multiply(own[n], rows[n], hidden, n == 0)
        else:
            multiply(other[n], rows[at_ref[n]], hidden, n == 0)
        if k == per - 1:
            total = project(hidden[...], factor[0], p_own[...])
    total = total + project(hidden[...], factor[1], p_other[...])
    half = total.shape[0] // 2
    count = total.shape[1] // NZ
    for n in range(NZ):
        part = total[:, n * count : (n + 1) * count]
        part = jnp.concatenate([part[:half], part[half:]], axis=1)
        out_ref[n * half : (n + 1) * half, :] = part.astype(BF16)


def sum_units(at, p_own, p_other, f_own, f_other, own, rows, weights):
    units, depth = own.shape
    tokens, width = f_own.shape[1], p_own.shape[1]
    deep = depth // NY
    copies = 2 * NY + 2 + len(weights)
    return pl.pallas_call(
        units_kernel,
        in_specs=[SMEM, VMEM, VMEM] + [HBM] * (4 + len(weights)),
        out_specs=VMEM,
        out_shape=jax.ShapeDtypeStruct((NZ * width // 2, 2 * tokens // NZ), BF16),
        scratch_shapes=[
            pltpu.VMEM((NY, tokens, deep), BF16),
            pltpu.VMEM((NY, units, deep), BF16),
            pltpu.VMEM((NY, units, deep), BF16),
            pltpu.VMEM((2, units, tokens), BF16),
            pltpu.VMEM((units, tokens), F32),
            pltpu.SemaphoreType.DMA((copies,)),
        ],
        compiler_params=pltpu.CompilerParams(vmem_limit_bytes=56 * 1024 * 1024),
        cost_estimate=SMALL,
        name="sum_units",
    )(at, p_own, p_other, f_own, f_other, own, rows, *weights)


def together(*arrays):
    return lax.optimization_barrier(arrays)


def body(upstream, inputs, gate_pre, up_pre, down_weight, proj_in, proj_out, queries, owner_table):
    rows_own = upstream[0]
    count, depth = rows_own.shape
    units = down_weight.shape[0]
    tp, sc = lax.axis_index("tp"), lax.axis_index("sc")
    x_lo, z = tp // NZ, tp % NZ
    x_hi, y, core = sc // (2 * NY), (sc // 2) % NY, sc % 2

    columns = [list(range(NZ)), list(range(NZ, 2 * NZ))]

    piece = depth // (2 * NY)
    rows = lax.all_gather(rows_own, "tp", axis=0, tiled=True, axis_index_groups=columns)

    def eighth(dy):
        column = (((y + dy) % NY) * 2 + core) * piece
        return lax.dynamic_slice(down_weight, (0, column), (units, piece))

    first, second = together(eighth(0), eighth(2))
    here = along_tp(first, 1, 0)
    other_queries, proj_other = across_x(queries), across_x(proj_out)

    in_factor = jnp.dot(inputs[0], proj_in, preferred_element_type=F32).astype(BF16)
    owners = owner_table[0, :, 0]
    ids = jnp.arange(count, dtype=jnp.int32)
    same = (owners[:, None] == owners[None, :]) & (ids[:, None] > ids[None, :])
    rank = jnp.sum(same.astype(jnp.int32), axis=1)
    groups = 2 * NY
    slot = (owners % groups) * (2 * CAP) + ((owners // groups) ^ x_hi) * CAP + rank
    slots = groups * 2 * CAP
    place = (slot[:, None] == jnp.arange(slots, dtype=jnp.int32)[None, :]).astype(BF16)
    packed = lax.dot_general(
        place,
        jnp.concatenate([in_factor, in_factor], axis=1),
        (((0,), (0,)), ((), ())),
        preferred_element_type=F32,
    ).astype(BF16)
    near = [list(range(groups)), list(range(groups, 2 * groups))]
    arrived = lax.all_to_all(
        packed, "sc", split_axis=0, concat_axis=0, tiled=True, axis_index_groups=near
    )

    gate, up_rows = gate_pre[0].T, up_pre[0].T
    factor_other = gating_factor(jnp.stack([1 - x_lo]), gate, up_rows)
    factor_own = gating_factor(jnp.stack([x_lo]), gate, up_rows)

    here, second, arrived, factor_other, factor_own = together(
        here, second, arrived, factor_other, factor_own
    )
    before, after = along_sc(here, 1, 0), along_sc(here, -1, 0)
    factor_other, far = along_tp(factor_other, 1, 0), across_x(second)
    mats = contract_queries(arrived, queries, other_queries)
    mats = lax.all_to_all(
        mats, "sc", split_axis=0, concat_axis=0, tiled=True, axis_index_groups=near
    )
    before, after, factor_other, far, proj_other, flipped = together(
        before, after, factor_other, far, proj_other, along_sc(here, 0, 1)
    )
    weights = [here, flipped]
    for a in (before, after, far):
        weights += [a, along_sc(a, 0, 1)]

    at = [(y + dy) % NY for dy in (0, -1, 1, 2)] + [core, 1 - core]
    parts = sum_units(
        jnp.stack(at).astype(jnp.int32),
        proj_out,
        proj_other,
        factor_own,
        factor_other,
        down_weight,
        rows,
        weights,
    )
    parts, mats = together(parts, mats)
    parts = lax.all_to_all(
        parts, "tp", split_axis=0, concat_axis=0, tiled=True, axis_index_groups=columns
    )
    return score_rows(place, mats, parts)[None]


def solution(mesh):
    placed = (
        P("sc", "tp", None),
        P("sc", "tp", None),
        P("sc", None, "tp"),
        P("sc", None, "tp"),
        P("tp", None),
        P(),
        P("tp", None),
        P("sc", None),
        P("sc", "tp", None),
    )
    return jax.shard_map(
        body, mesh=mesh, in_specs=placed, out_specs=P("sc", "tp", None), check_vma=False
    )
```
